256 devices in a mesh: dev: 256 (over x, z, y, core).
Axes of the slice: x: 4, y: 4, z: 8, core: 2. Of those that a mesh axis runs over, the one named last changes fastest.
Arguments:
- embeddings: bfloat16 [262144, 768], P('dev')
Outputs:
- keep_weight: float32 [262144], P('dev')
All inputs are finite; a program needn't handle non-finite values.
Results may differ from the reference program's by a relative error of at most 0.0044.
Values may be sent and summed in bfloat16 or wider, within the bound.
No kernel may reach another device: no remote copies, remote signals or barrier semaphores. Data moves between devices by JAX's collectives and lax.ppermute only.
A program may use at most 64 MiB of HBM per device.

```python
import math
import jax
import jax.numpy as jnp
import numpy as np
from jax import lax

D = 768
TILE = 1024
ROUNDS = 4
ROWS = 262144
N_DEV = 256


def draw_embeddings(key, part):
    key = jax.random.fold_in(key, 11)
    key_centers = jax.random.fold_in(key, 0)
    key_pick = jax.random.fold_in(key, 1)
    key_noise = jax.random.fold_in(key, 2)
    key_tight = jax.random.fold_in(key, 4)
    key_block = jax.random.fold_in(key, 5)
    blocks = ROWS // TILE
    clusters = blocks // 2 ** ROUNDS
    row_index = jnp.arange(ROWS, dtype=jnp.int32)
    block_index = row_index // TILE
    cluster_index = block_index % clusters
    limit = TILE - 3 * TILE * block_index // (4 * blocks)
    local_pick = jax.random.randint(key_pick, (ROWS,), 0, limit)
    center_index = cluster_index * TILE + local_pick
    block_draw = jax.random.uniform(key_block, (blocks,), jnp.float32)
    block_loose = block_draw[block_index]
    spread = jax.random.uniform(key_tight, (ROWS,), jnp.float32)
    centers = jax.random.normal(key_centers, (clusters * TILE, D), jnp.float32)
    noise = jax.random.normal(key_noise, (ROWS, D), jnp.float32)
    looseness = (0.004 + 0.33 * block_loose ** 5) * jnp.exp(-2.0 * spread)
    closeness = 1.0 - looseness
    across = jnp.sqrt(looseness * (2.0 - looseness))
    values = closeness[:, None] * centers[center_index] + across[:, None] * noise
    return values.astype(jnp.bfloat16)


def setup_inputs(seed: int = 0) -> dict:
    seeds = jax.random.split(jax.random.key(seed), 2)
    embeddings = draw_embeddings(jax.random.fold_in(seeds[1], 71), 0)
    return {"embeddings": embeddings}


sharpness = 10.0

def normalize(values):
    widened = values.astype(jnp.float32)
    scaled = widened * lax.rsqrt(lax.optimization_barrier(jnp.mean(widened * widened, axis=1, keepdims=True)) + 1e-06) / math.sqrt(values.shape[1])
    return scaled.astype(jnp.bfloat16)

def kernel_tile(left, right):
    similarity = jnp.dot(left, right.T, preferred_element_type=jnp.float32)
    return jnp.exp(sharpness * (similarity - 1.0))

def self_sums(block):
    return lax.optimization_barrier(jnp.sum(kernel_tile(block, block), axis=1))

def pair_sums(pair):
    tile_values = kernel_tile(pair[0], pair[1])
    return (lax.optimization_barrier(jnp.sum(tile_values, axis=1)), lax.optimization_barrier(jnp.sum(tile_values, axis=0)))

def reference(embeddings):
    normed = normalize(embeddings)
    blocks = normed.reshape(N_DEV, TILE, normed.shape[1])
    density = lax.map(self_sums, blocks)
    levels = N_DEV.bit_length() - 1
    players = np.arange(N_DEV)
    for round_index in range(ROUNDS):
        stride = 1 << levels - 1 - round_index
        lower = jnp.asarray(players[players & stride == 0], dtype=jnp.int32)
        upper = lower + stride
        row_sums, column_sums = lax.map(pair_sums, (blocks[lower], blocks[upper]))
        density = density.at[lower].add(row_sums).at[upper].add(column_sums)
    weights = 1.0 / density
    total = jnp.sum(weights)
    return (weights * (N_DEV * TILE) / total).reshape(N_DEV * TILE)
```

```python
import math

import jax
import jax.numpy as jnp
import numpy as np
from jax import lax
from jax.sharding import PartitionSpec as P

ROUNDS = 4


sharpness = 10.0


def parity(value):
    return bin(value).count("1") & 1


def plan(players):
    low = players.bit_length() - 1 - ROUNDS
    z_near, z_swap = 1 << low, 3 << low
    x_near, x_swap = 4 << low, 12 << low
    first, second = [], []
    for player in range(players):
        if parity(player >> low) ^ (player & 1):
            first.append((player, player ^ x_near))
            second.append((player, player ^ z_swap))
        else:
            first.append((player, player ^ z_near))
            second.append((player, player ^ x_swap))
    return first, second


def inverse(pairs):
    return [(target, source) for source, target in pairs]


def normalize(values):
    widened = values.astype(jnp.float32)
    scaled = (
        widened
        * lax.rsqrt(jnp.mean(widened * widened, axis=1, keepdims=True) + 1e-06)
        / math.sqrt(values.shape[1])
    )
    return scaled.astype(jnp.bfloat16)


def kernel_tile(left, right):
    similarity = lax.dot_general(
        left, right, (((1,), (1,)), ((), ())), preferred_element_type=jnp.float32
    )
    return jnp.exp(sharpness * (similarity - 1.0))


def shards(embeddings):
    players = lax.axis_size("dev")
    rows = embeddings.shape[0]
    first, second = plan(players)
    near = lax.ppermute(embeddings, "dev", first)
    far = lax.ppermute(embeddings, "dev", second)
    own = normalize(embeddings)
    near = normalize(near)
    far = normalize(far)
    density = jnp.sum(kernel_tile(own, own), axis=1)
    own_near = kernel_tile(own, near)
    near_far = kernel_tile(near, far)
    to_near = jnp.sum(own_near, axis=0) + jnp.sum(near_far, axis=1)
    to_far = jnp.sum(near_far, axis=0)
    density = density + jnp.sum(own_near, axis=1)
    density = density + lax.ppermute(to_near, "dev", inverse(first))
    density = density + lax.ppermute(to_far, "dev", inverse(second))
    weights = 1.0 / density
    totals = lax.all_to_all(
        jnp.full((players, 128), jnp.sum(weights)), "dev", 0, 0, tiled=True
    )
    total = jnp.sum(totals[:, 0])
    return weights * (players * rows) / total


def solution(mesh):
    return jax.shard_map(
        shards,
        mesh=mesh,
        in_specs=(P("dev", None),),
        out_specs=P("dev"),
        check_vma=False,
    )
```

```python
import functools
import math

import jax
import jax.numpy as jnp
from jax import lax
from jax.experimental import pallas as pl
from jax.experimental.pallas import tpu as pltpu
from jax.sharding import PartitionSpec as P

ROUNDS = 4
LANES = 128
STEP = 256
LATE = 768

sharpness = 10.0
RATE = sharpness * math.log2(math.e)


def parity(value):
    return bin(value).count("1") & 1


def plan(players):
    low = players.bit_length() - 1 - ROUNDS
    z_near, z_swap = 1 << low, 3 << low
    x_near, x_swap = 4 << low, 12 << low
    near, far = ([], []), ([], [])
    for player in range(players):
        odd = (player >> (low - 1)) & 1
        if parity(player >> low) ^ (player & 1):
            near[1 - odd].append((player, player ^ x_near))
            far[odd].append((player, player ^ z_swap))
        else:
            near[odd].append((player, player ^ z_near))
            far[1 - odd].append((player, player ^ x_swap))
    return near, far


def inverse(pairs):
    return [(target, source) for source, target in pairs]


def is_late():
    me = lax.axis_index("dev")
    bits = me ^ (me >> 3) ^ (me >> 4) ^ (me >> 5) ^ (me >> 6) ^ (me >> 7)
    return lax.rem(bits, 2) == 0


def unit(values):
    widened = values.astype(jnp.float32)
    mean = jnp.mean(widened * widened, axis=1, keepdims=True)
    scale = lax.rsqrt(mean + 1e-06) * (1.0 / math.sqrt(values.shape[1]))
    return (widened * scale).astype(jnp.bfloat16)


def unit_rows(source, target):
    rows = source.shape[0]
    for start in range(0, rows, STEP):
        part = pl.ds(start, min(STEP, rows - start))
        target[part, :] = unit(source[part, :])


def put(target, start, vector, add):
    for k in range(vector.shape[1] // LANES):
        at = pl.ds(start // LANES + k, 1)
        part = vector[:, k * LANES : (k + 1) * LANES]
        target[at, :] = target[at, :] + part if add else part


def tile_sums(left, right, row_out, row_start, row_add, col_out, col_start, col_add):
    rows, cols = left.shape[0], right.shape[0]
    total = None
    for start in range(0, rows, STEP):
        similarity = lax.dot_general(
            left[pl.ds(start, STEP), :],
            right[...],
            (((1,), (1,)), ((), ())),
            preferred_element_type=jnp.float32,
        )
        value = jnp.exp2(similarity * RATE - RATE)
        folded = value[:, :LANES]
        for k in range(1, cols // LANES):
            folded = folded + value[:, k * LANES : (k + 1) * LANES]
        sums = jnp.sum(folded.T, axis=0, keepdims=True)
        put(row_out, row_start + start, sums, row_add)
        if col_out is not None:
            part = jnp.sum(value.reshape(STEP // 8, 8, cols), axis=0)
            total = part if total is None else total + part
    if col_out is not None:
        put(col_out, col_start, jnp.sum(total, axis=0, keepdims=True), col_add)


def own_kernel(raw, normed, first, second, density):
    unit_rows(raw, normed)
    first[...] = raw[pl.ds(0, LATE), :]
    second[...] = raw[pl.ds(LATE, raw.shape[0] - LATE), :]
    tile_sums(normed, normed, density, 0, False, None, 0, False)


def early_kernel(normed, near_raw, far_raw, density, density_out, to_near, to_far, near, far):
    density_out[...] = density[...]

    @pl.when(jnp.logical_not(is_late()))
    def _():
        unit_rows(near_raw, near)
        unit_rows(far_raw, far)
        tile_sums(normed, near, density_out, 0, True, to_near, 0, False)
        tile_sums(near, far, to_near, 0, True, to_far, 0, False)


def late_first_kernel(
    normed, near_raw, far_raw, density, to_near, to_far,
    density_out, near_out, far_out, near, far,
):
    density_out[...] = density[...]
    near_out[...] = to_near[...]
    far_out[...] = to_far[...]

    @pl.when(is_late())
    def _():
        unit_rows(near_raw, near)
        unit_rows(far_raw, far)
        tile_sums(normed, near, density_out, 0, True, near_out, 0, False)
        tile_sums(near, far, near_out, 0, True, far_out, 0, False)


def late_second_kernel(
    normed, near_first, far_first, near_raw, far_raw, density, to_near, to_far,
    density_out, near_out, far_out, near, far,
):
    density_out[...] = density[...]
    near_out[...] = to_near[...]
    far_out[...] = to_far[...]

    @pl.when(is_late())
    def _():
        unit_rows(near_raw, near)
        unit_rows(far_raw, far)
        tile_sums(normed, near, density_out, 0, True, near_out, LATE, False)
        tile_sums(near_first, far, near_out, 0, True, far_out, LATE, False)
        tile_sums(near, far_first, near_out, LATE, True, far_out, 0, True)
        tile_sums(near, far, near_out, LATE, True, far_out, LATE, True)


def weight_kernel(density, from_near, from_far, weights, total):
    value = 1.0 / (density[...] + from_near[...] + from_far[...])
    weights[...] = value
    total[...] = jnp.full(total.shape, jnp.sum(value))


def scale_kernel(weights, totals, keep, *, rows):
    total = jnp.sum(totals[...], axis=0, keepdims=True)
    keep[...] = weights[...] * rows / total


def call(kernel, operands, outs, scratch=(), flops=0):
    space = pl.BlockSpec(memory_space=pltpu.VMEM)
    shapes = [jax.ShapeDtypeStruct(*out) for out in outs]
    moved = sum(math.prod(s.shape) * s.dtype.itemsize for s in [*operands, *shapes])
    return pl.pallas_call(
        kernel,
        out_shape=shapes,
        in_specs=[space] * len(operands),
        out_specs=[space] * len(shapes),
        scratch_shapes=[pltpu.VMEM(*s) for s in scratch],
        cost_estimate=pl.CostEstimate(
            flops=flops, bytes_accessed=moved, transcendentals=0
        ),
        compiler_params=pltpu.CompilerParams(vmem_limit_bytes=32 * 2**20),
    )(*operands)


def shards(embeddings):
    players = lax.axis_size("dev")
    rows, width = embeddings.shape
    rest = rows - LATE
    bf16, f32 = jnp.bfloat16, jnp.float32
    sums = ((rows // LANES, LANES), f32)
    tile = 2 * rows * rows * width
    near, far = plan(players)

    near_early = lax.ppermute(embeddings, "dev", near[0])
    far_early = lax.ppermute(embeddings, "dev", far[0])
    normed, first, second, density = call(
        own_kernel,
        [embeddings],
        [((rows, width), bf16), ((LATE, width), bf16), ((rest, width), bf16), sums],
        flops=tile,
    )
    near_first = lax.ppermute(first, "dev", near[1])
    far_first = lax.ppermute(first, "dev", far[1])
    near_second = lax.ppermute(second, "dev", near[1])
    far_second = lax.ppermute(second, "dev", far[1])

    density, to_near, to_far = call(
        early_kernel,
        [normed, near_early, far_early, density],
        [sums, sums, sums],
        [((rows, width), bf16)] * 2,
        flops=2 * tile,
    )
    density, to_near, to_far, near_first, far_first = call(
        late_first_kernel,
        [normed, near_first, far_first, density, to_near, to_far],
        [sums, sums, sums] + [((LATE, width), bf16)] * 2,
        flops=tile * 21 // 16,
    )
    density, to_near, to_far = call(
        late_second_kernel,
        [normed, near_first, far_first, near_second, far_second, density, to_near, to_far],
        [sums, sums, sums],
        [((rest, width), bf16)] * 2,
        flops=tile * 11 // 16,
    )
    from_near = lax.ppermute(to_near, "dev", inverse(near[0] + near[1]))
    from_far = lax.ppermute(to_far, "dev", inverse(far[0] + far[1]))
    weights, total = call(
        weight_kernel, [density, from_near, from_far], [sums, ((players, LANES), f32)]
    )
    totals = lax.all_to_all(total, "dev", 0, 0, tiled=True)
    (keep,) = call(
        functools.partial(scale_kernel, rows=float(players * rows)), [weights, totals], [sums]
    )
    return keep.reshape(rows)


def solution(mesh):
    return jax.shard_map(
        shards,
        mesh=mesh,
        in_specs=(P("dev", None),),
        out_specs=P("dev"),
        check_vma=False,
    )
```

```python
import functools
import math

import jax
import jax.numpy as jnp
from jax import lax
from jax.experimental import pallas as pl
from jax.experimental.pallas import tpu as pltpu
from jax.sharding import PartitionSpec as P

ROUNDS = 4
LANES = 128
STEP = 256
LATE = 768

sharpness = 10.0
RATE = sharpness * math.log2(math.e)


def parity(value):
    return bin(value).count("1") & 1


def plan(players):
    low = players.bit_length() - 1 - ROUNDS
    z_near, z_swap = 1 << low, 3 << low
    x_near, x_swap = 4 << low, 12 << low
    near, far = ([], []), ([], [])
    for player in range(players):
        odd = (player >> (low - 1)) & 1
        if parity(player >> low) ^ (player & 1):
            near[1 - odd].append((player, player ^ x_near))
            far[odd].append((player, player ^ z_swap))
        else:
            near[odd].append((player, player ^ z_near))
            far[1 - odd].append((player, player ^ x_swap))
    return near, far


def inverse(pairs):
    return [(target, source) for source, target in pairs]


def is_late():
    me = lax.axis_index("dev")
    bits = me ^ (me >> 3) ^ (me >> 4) ^ (me >> 5) ^ (me >> 6) ^ (me >> 7)
    return lax.rem(bits, 2) == 0


def unit(values):
    widened = values.astype(jnp.float32)
    mean = jnp.mean(widened * widened, axis=1, keepdims=True)
    scale = lax.rsqrt(mean + 1e-06) * (1.0 / math.sqrt(values.shape[1]))
    return (widened * scale).astype(jnp.bfloat16)


def unit_rows(source, target):
    rows = source.shape[0]
    for start in range(0, rows, STEP):
        part = pl.ds(start, min(STEP, rows - start))
        target[part, :] = unit(source[part, :])


def put(target, start, vector, add):
    for k in range(vector.shape[1] // LANES):
        at = pl.ds(start // LANES + k, 1)
        part = vector[:, k * LANES : (k + 1) * LANES]
        target[at, :] = target[at, :] + part if add else part


def tile_sums(left, right, row_out, row_start, row_add, col_out, col_start, col_add):
    rows, cols = left.shape[0], right.shape[0]
    total = None
    for start in range(0, rows, STEP):
        similarity = lax.dot_general(
            left[pl.ds(start, STEP), :],
            right[...],
            (((1,), (1,)), ((), ())),
            preferred_element_type=jnp.float32,
        )
        value = jnp.exp2(similarity * RATE - RATE)
        folded = value[:, :LANES]
        for k in range(1, cols // LANES):
            folded = folded + value[:, k * LANES : (k + 1) * LANES]
        sums = jnp.sum(folded.T, axis=0, keepdims=True)
        put(row_out, row_start + start, sums, row_add)
        if col_out is not None:
            part = jnp.sum(value.reshape(STEP // 8, 8, cols), axis=0)
            total = part if total is None else total + part
    if col_out is not None:
        put(col_out, col_start, jnp.sum(total, axis=0, keepdims=True), col_add)


def gate_kernel(raw, arrived, density, first, second):
    first[...] = raw[pl.ds(0, LATE), :]
    second[...] = raw[pl.ds(LATE, raw.shape[0] - LATE), :]


def own_kernel(raw, normed, density):
    unit_rows(raw, normed)
    tile_sums(normed, normed, density, 0, False, None, 0, False)


def early_kernel(normed, near_raw, far_raw, density, density_out, to_near, to_far, near, far):
    density_out[...] = density[...]

    @pl.when(jnp.logical_not(is_late()))
    def _():
        unit_rows(near_raw, near)
        unit_rows(far_raw, far)
        tile_sums(normed, near, density_out, 0, True, to_near, 0, False)
        tile_sums(near, far, to_near, 0, True, to_far, 0, False)


def late_first_kernel(
    normed, near_raw, far_raw, density, to_near, to_far,
    density_out, near_out, far_out, near, far,
):
    density_out[...] = density[...]
    near_out[...] = to_near[...]
    far_out[...] = to_far[...]

    @pl.when(is_late())
    def _():
        unit_rows(near_raw, near)
        unit_rows(far_raw, far)
        tile_sums(normed, near, density_out, 0, True, near_out, 0, False)
        tile_sums(near, far, near_out, 0, True, far_out, 0, False)


def late_second_kernel(
    normed, near_first, far_first, near_raw, far_raw, density, to_near, to_far,
    density_out, near_out, far_out, near, far,
):
    density_out[...] = density[...]
    near_out[...] = to_near[...]
    far_out[...] = to_far[...]

    @pl.when(is_late())
    def _():
        unit_rows(near_raw, near)
        unit_rows(far_raw, far)
        tile_sums(normed, near, density_out, 0, True, near_out, LATE, False)
        tile_sums(near_first, far, near_out, 0, True, far_out, LATE, False)
        tile_sums(near, far_first, near_out, LATE, True, far_out, 0, True)
        tile_sums(near, far, near_out, LATE, True, far_out, LATE, True)


def weight_kernel(density, from_near, from_far, weights, total):
    value = 1.0 / (density[...] + from_near[...] + from_far[...])
    weights[...] = value
    total[...] = jnp.full(total.shape, jnp.sum(value))


def scale_kernel(weights, totals, keep, *, rows):
    total = jnp.sum(totals[...], axis=0, keepdims=True)
    keep[...] = weights[...] * rows / total


def call(kernel, operands, outs, scratch=(), flops=0, whole=()):
    space = pl.BlockSpec(memory_space=pltpu.VMEM)
    anywhere = pl.BlockSpec(memory_space=pl.ANY)
    shapes = [jax.ShapeDtypeStruct(*out) for out in outs]
    moved = sum(math.prod(s.shape) * s.dtype.itemsize for s in [*operands, *shapes])
    return pl.pallas_call(
        kernel,
        out_shape=shapes,
        in_specs=[anywhere if i in whole else space for i in range(len(operands))],
        out_specs=[space] * len(shapes),
        scratch_shapes=[pltpu.VMEM(*s) for s in scratch],
        cost_estimate=pl.CostEstimate(
            flops=flops, bytes_accessed=moved, transcendentals=0
        ),
        compiler_params=pltpu.CompilerParams(vmem_limit_bytes=32 * 2**20),
    )(*operands)


def shards(embeddings):
    players = lax.axis_size("dev")
    rows, width = embeddings.shape
    rest = rows - LATE
    bf16, f32 = jnp.bfloat16, jnp.float32
    sums = ((rows // LANES, LANES), f32)
    tile = 2 * rows * rows * width
    near, far = plan(players)

    near_early = lax.ppermute(embeddings, "dev", near[0])
    far_early = lax.ppermute(embeddings, "dev", far[0])
    normed, density = call(
        own_kernel, [embeddings], [((rows, width), bf16), sums], flops=tile
    )
    first, second = call(
        gate_kernel,
        [embeddings, near_early, density],
        [((LATE, width), bf16), ((rest, width), bf16)],
        whole=(1, 2),
    )
    near_first = lax.ppermute(first, "dev", near[1])
    far_first = lax.ppermute(first, "dev", far[1])
    near_second = lax.ppermute(second, "dev", near[1])
    far_second = lax.ppermute(second, "dev", far[1])

    density, to_near, to_far = call(
        early_kernel,
        [normed, near_early, far_early, density],
        [sums, sums, sums],
        [((rows, width), bf16)] * 2,
        flops=2 * tile,
    )
    density, to_near, to_far, near_first, far_first = call(
        late_first_kernel,
        [normed, near_first, far_first, density, to_near, to_far],
        [sums, sums, sums] + [((LATE, width), bf16)] * 2,
        flops=tile * 21 // 16,
    )
    density, to_near, to_far = call(
        late_second_kernel,
        [normed, near_first, far_first, near_second, far_second, density, to_near, to_far],
        [sums, sums, sums],
        [((rest, width), bf16)] * 2,
        flops=tile * 11 // 16,
    )
    from_near = lax.ppermute(to_near, "dev", inverse(near[0] + near[1]))
    from_far = lax.ppermute(to_far, "dev", inverse(far[0] + far[1]))
    weights, total = call(
        weight_kernel, [density, from_near, from_far], [sums, ((players, LANES), f32)]
    )
    totals = lax.all_to_all(total, "dev", 0, 0, tiled=True)
    (keep,) = call(
        functools.partial(scale_kernel, rows=float(players * rows)), [weights, totals], [sums]
    )
    return keep.reshape(rows)


def solution(mesh):
    return jax.shard_map(
        shards,
        mesh=mesh,
        in_specs=(P("dev", None),),
        out_specs=P("dev"),
        check_vma=False,
    )
```

```python
import functools
import math

import jax
import jax.numpy as jnp
from jax import lax
from jax.experimental import pallas as pl
from jax.experimental.pallas import tpu as pltpu
from jax.sharding import PartitionSpec as P

ROUNDS = 4
LANES = 128
STEP = 256

sharpness = 10.0
RATE = sharpness * math.log2(math.e)


def parity(value):
    return bin(value).count("1") & 1


def plan(players):
    low = players.bit_length() - 1 - ROUNDS
    z_near, z_swap = 1 << low, 3 << low
    x_near, x_swap = 4 << low, 12 << low
    near, far = [], []
    for player in range(players):
        if parity(player >> low) ^ (player & 1):
            near.append((player, player ^ x_near))
            far.append((player, player ^ z_swap))
        else:
            near.append((player, player ^ z_near))
            far.append((player, player ^ x_swap))
    return near, far


def inverse(pairs):
    return [(target, source) for source, target in pairs]


def unit(values):
    widened = values.astype(jnp.float32)
    mean = jnp.mean(widened * widened, axis=1, keepdims=True)
    scale = lax.rsqrt(mean + 1e-06) * (1.0 / math.sqrt(values.shape[1]))
    return (widened * scale).astype(jnp.bfloat16)


def unit_rows(source, target):
    rows = source.shape[0]
    for start in range(0, rows, STEP):
        part = pl.ds(start, min(STEP, rows - start))
        target[part, :] = unit(source[part, :])


def put(target, start, vector, add):
    for k in range(vector.shape[1] // LANES):
        at = pl.ds(start // LANES + k, 1)
        part = vector[:, k * LANES : (k + 1) * LANES]
        target[at, :] = target[at, :] + part if add else part


def tile_sums(left, right, row_out, row_start, row_add, col_out, col_start, col_add):
    rows, cols = left.shape[0], right.shape[0]
    total = None
    for start in range(0, rows, STEP):
        similarity = lax.dot_general(
            left[pl.ds(start, STEP), :],
            right[...],
            (((1,), (1,)), ((), ())),
            preferred_element_type=jnp.float32,
        )
        value = jnp.exp2(similarity * RATE - RATE)
        folded = value[:, :LANES]
        for k in range(1, cols // LANES):
            folded = folded + value[:, k * LANES : (k + 1) * LANES]
        sums = jnp.sum(folded.T, axis=0, keepdims=True)
        put(row_out, row_start + start, sums, row_add)
        if col_out is not None:
            part = jnp.sum(value.reshape(STEP // 8, 8, cols), axis=0)
            total = part if total is None else total + part
    if col_out is not None:
        put(col_out, col_start, jnp.sum(total, axis=0, keepdims=True), col_add)


def own_kernel(raw, normed, density):
    unit_rows(raw, normed)
    tile_sums(normed, normed, density, 0, False, None, 0, False)


def near_kernel(normed, raw, density, density_out, to_near, near):
    unit_rows(raw, near)
    density_out[...] = density[...]
    tile_sums(normed, near, density_out, 0, True, to_near, 0, False)


def far_kernel(near, raw, to_near, near_out, to_far, far):
    unit_rows(raw, far)
    near_out[...] = to_near[...]
    tile_sums(near, far, near_out, 0, True, to_far, 0, False)


def weight_kernel(density, from_near, from_far, weights, total):
    value = 1.0 / (density[...] + from_near[...] + from_far[...])
    weights[...] = value
    total[...] = jnp.full(total.shape, jnp.sum(value))


def scale_kernel(weights, totals, keep, *, rows):
    total = jnp.sum(totals[...], axis=0, keepdims=True)
    keep[...] = weights[...] * rows / total


def call(kernel, operands, outs, scratch=(), flops=0):
    space = pl.BlockSpec(memory_space=pltpu.VMEM)
    shapes = [jax.ShapeDtypeStruct(*out) for out in outs]
    moved = sum(math.prod(s.shape) * s.dtype.itemsize for s in [*operands, *shapes])
    return pl.pallas_call(
        kernel,
        out_shape=shapes,
        in_specs=[space] * len(operands),
        out_specs=[space] * len(shapes),
        scratch_shapes=[pltpu.VMEM(*s) for s in scratch],
        cost_estimate=pl.CostEstimate(
            flops=flops, bytes_accessed=moved, transcendentals=0
        ),
        compiler_params=pltpu.CompilerParams(vmem_limit_bytes=32 * 2**20),
    )(*operands)


def shards(embeddings):
    players = lax.axis_size("dev")
    rows, width = embeddings.shape
    bf16, f32 = jnp.bfloat16, jnp.float32
    block, sums = ((rows, width), bf16), ((rows // LANES, LANES), f32)
    tile = 2 * rows * rows * width
    near_pairs, far_pairs = plan(players)

    near = lax.ppermute(embeddings, "dev", near_pairs)
    far = lax.ppermute(embeddings, "dev", far_pairs)
    normed, density = call(own_kernel, [embeddings], [block, sums], flops=tile)
    density, to_near, near = call(
        near_kernel, [normed, near, density], [sums, sums, block], flops=tile
    )
    to_near, to_far = call(
        far_kernel, [near, far, to_near], [sums, sums], [block], flops=tile
    )
    from_near = lax.ppermute(to_near, "dev", inverse(near_pairs))
    from_far = lax.ppermute(to_far, "dev", inverse(far_pairs))
    weights, total = call(
        weight_kernel, [density, from_near, from_far], [sums, ((players, LANES), f32)]
    )
    totals = lax.all_to_all(total, "dev", 0, 0, tiled=True)
    (keep,) = call(
        functools.partial(scale_kernel, rows=float(players * rows)), [weights, totals], [sums]
    )
    return keep.reshape(rows)


def solution(mesh):
    return jax.shard_map(
        shards,
        mesh=mesh,
        in_specs=(P("dev", None),),
        out_specs=P("dev"),
        check_vma=False,
    )
```

```python
import functools
import math

import jax
import jax.numpy as jnp
from jax import lax
from jax.experimental import pallas as pl
from jax.experimental.pallas import tpu as pltpu
from jax.sharding import PartitionSpec as P

ROUNDS = 4
LANES = 128
STEP = 256

sharpness = 10.0
RATE = sharpness * math.log2(math.e)


def parity(value):
    return bin(value).count("1") & 1


def plan(players):
    low = players.bit_length() - 1 - ROUNDS
    z_near, z_swap = 1 << low, 3 << low
    x_near, x_swap = 4 << low, 12 << low
    pairs = [], [], [], []
    for player in range(players):
        z_holder = parity(player >> low) ^ (player & 1)
        pairs[0 if not z_holder else 2].append((player, player ^ (x_near if z_holder else z_near)))
        pairs[1 if z_holder else 3].append((player, player ^ (z_swap if z_holder else x_swap)))
    return pairs


def inverse(pairs):
    return [(target, source) for source, target in pairs]


def holds_z():
    me = lax.axis_index("dev")
    bits = me ^ (me >> 4) ^ (me >> 5) ^ (me >> 6) ^ (me >> 7)
    return lax.rem(bits, 2) == 1


def unit(values):
    widened = values.astype(jnp.float32)
    mean = jnp.mean(widened * widened, axis=1, keepdims=True)
    scale = lax.rsqrt(mean + 1e-06) * (1.0 / math.sqrt(values.shape[1]))
    return (widened * scale).astype(jnp.bfloat16)


def unit_rows(source, target):
    rows = source.shape[0]
    for start in range(0, rows, STEP):
        part = pl.ds(start, min(STEP, rows - start))
        target[part, :] = unit(source[part, :])


def put(target, start, vector, add):
    for k in range(vector.shape[1] // LANES):
        at = pl.ds(start // LANES + k, 1)
        part = vector[:, k * LANES : (k + 1) * LANES]
        target[at, :] = target[at, :] + part if add else part


def tile_sums(left, right, row_out, row_start, row_add, col_out, col_start, col_add):
    rows, cols = left.shape[0], right.shape[0]
    total = None
    for start in range(0, rows, STEP):
        similarity = lax.dot_general(
            left[pl.ds(start, STEP), :],
            right[...],
            (((1,), (1,)), ((), ())),
            preferred_element_type=jnp.float32,
        )
        value = jnp.exp2(similarity * RATE - RATE)
        folded = value[:, :LANES]
        for k in range(1, cols // LANES):
            folded = folded + value[:, k * LANES : (k + 1) * LANES]
        sums = jnp.sum(folded.T, axis=0, keepdims=True)
        put(row_out, row_start + start, sums, row_add)
        if col_out is not None:
            part = jnp.sum(value.reshape(STEP // 8, 8, cols), axis=0)
            total = part if total is None else total + part
    if col_out is not None:
        put(col_out, col_start, jnp.sum(total, axis=0, keepdims=True), col_add)


def own_kernel(raw, normed, density):
    unit_rows(raw, normed)
    tile_sums(normed, normed, density, 0, False, None, 0, False)


def x_kernel(normed, near_raw, far_raw, density, density_out, to_near, to_far, near, far):
    density_out[...] = density[...]

    @pl.when(jnp.logical_not(holds_z()))
    def _():
        unit_rows(near_raw, near)
        unit_rows(far_raw, far)
        tile_sums(normed, near, density_out, 0, True, to_near, 0, False)
        tile_sums(near, far, to_near, 0, True, to_far, 0, False)

    @pl.when(holds_z())
    def _():
        to_near[...] = jnp.zeros_like(to_near)
        to_far[...] = jnp.zeros_like(to_far)


def add_kernel(first, second, third, out):
    out[...] = first[...] + second[...] + third[...]


def near_kernel(raw, part, near):
    @pl.when(holds_z())
    def _():
        unit_rows(raw, near)


def far_kernel(near, raw, part, part_out, to_far, far):
    part_out[...] = part[...]

    @pl.when(holds_z())
    def _():
        unit_rows(raw, far)
        tile_sums(near, far, part_out, 0, True, to_far, 0, False)


def own_near_kernel(normed, near, density, part, density_out, part_out):
    density_out[...] = density[...]
    part_out[...] = part[...]

    @pl.when(holds_z())
    def _():
        tile_sums(normed, near, density_out, 0, True, part_out, 0, True)


def weight_kernel(density, part, from_far, weights, near_weights, total):
    own = 1.0 / (density[...] + from_far[...])
    weights[...] = own

    @pl.when(holds_z())
    def _():
        near = 1.0 / part[...]
        near_weights[...] = near
        total[...] = jnp.full(total.shape, jnp.sum(own + near))

    @pl.when(jnp.logical_not(holds_z()))
    def _():
        near_weights[...] = jnp.zeros_like(near_weights)
        total[...] = jnp.zeros_like(total)


def scale_kernel(weights, sent_weights, totals, keep, *, rows):
    total = jnp.sum(totals[...], axis=0, keepdims=True)
    value = jnp.where(holds_z(), weights[...], sent_weights[...])
    keep[...] = value * rows / total


def call(kernel, operands, outs, scratch=(), flops=0):
    space = pl.BlockSpec(memory_space=pltpu.VMEM)
    shapes = [jax.ShapeDtypeStruct(*out) for out in outs]
    moved = sum(math.prod(s.shape) * s.dtype.itemsize for s in [*operands, *shapes])
    return pl.pallas_call(
        kernel,
        out_shape=shapes,
        in_specs=[space] * len(operands),
        out_specs=[space] * len(shapes),
        scratch_shapes=[pltpu.VMEM(*s) for s in scratch],
        cost_estimate=pl.CostEstimate(
            flops=flops, bytes_accessed=moved, transcendentals=0
        ),
        compiler_params=pltpu.CompilerParams(vmem_limit_bytes=32 * 2**20),
    )(*operands)


def shards(embeddings):
    players = lax.axis_size("dev")
    rows, width = embeddings.shape
    bf16, f32 = jnp.bfloat16, jnp.float32
    block, sums = ((rows, width), bf16), ((rows // LANES, LANES), f32)
    tile = 2 * rows * rows * width
    z_near, z_swap, x_near, x_swap = plan(players)

    near = lax.ppermute(embeddings, "dev", z_near)
    far = lax.ppermute(embeddings, "dev", z_swap)
    x_first = lax.ppermute(embeddings, "dev", x_near)
    x_second = lax.ppermute(embeddings, "dev", x_swap)
    normed, density = call(own_kernel, [embeddings], [block, sums], flops=tile)

    density, to_near, to_far = call(
        x_kernel,
        [normed, x_first, x_second, density],
        [sums, sums, sums],
        [block, block],
        flops=2 * tile,
    )
    from_near = lax.ppermute(to_near, "dev", inverse(x_near))
    from_far = lax.ppermute(to_far, "dev", inverse(x_swap))
    (density,) = call(add_kernel, [density, from_near, from_far], [sums])
    part = lax.ppermute(density, "dev", z_near)

    (near,) = call(near_kernel, [near, part], [block])
    part, to_far = call(far_kernel, [near, far, part], [sums, sums], [block], flops=tile)
    from_far = lax.ppermute(to_far, "dev", z_swap)
    density, part = call(
        own_near_kernel, [normed, near, density, part], [sums, sums], flops=tile
    )
    weights, near_weights, total = call(
        weight_kernel,
        [density, part, from_far],
        [sums, sums, ((players, LANES), f32)],
    )
    sent_weights = lax.ppermute(near_weights, "dev", inverse(z_near))
    totals = lax.all_to_all(total, "dev", 0, 0, tiled=True)
    (keep,) = call(
        functools.partial(scale_kernel, rows=float(players * rows)),
        [weights, sent_weights, totals],
        [sums],
    )
    return keep.reshape(rows)


def solution(mesh):
    return jax.shard_map(
        shards,
        mesh=mesh,
        in_specs=(P("dev", None),),
        out_specs=P("dev"),
        check_vma=False,
    )
```

```python
import functools
import math

import jax
import jax.numpy as jnp
from jax import lax
from jax.experimental import pallas as pl
from jax.experimental.pallas import tpu as pltpu
from jax.sharding import PartitionSpec as P

ROUNDS = 4
LANES = 128
STEP = 256

sharpness = 10.0
RATE = sharpness * math.log2(math.e)


def parity(value):
    return bin(value).count("1") & 1


def plan(players):
    low = players.bit_length() - 1 - ROUNDS
    z_near, z_swap = 1 << low, 3 << low
    x_near, x_swap = 4 << low, 12 << low
    near, far = [], []
    for player in range(players):
        if parity(player >> low) ^ (player & 1):
            near.append((player, player ^ x_near))
            far.append((player, player ^ z_swap))
        else:
            near.append((player, player ^ z_near))
            far.append((player, player ^ x_swap))
    return near, far


def inverse(pairs):
    return [(target, source) for source, target in pairs]


def unit(values):
    widened = values.astype(jnp.float32)
    mean = jnp.mean(widened * widened, axis=1, keepdims=True)
    scale = lax.rsqrt(mean + 1e-06) * (1.0 / math.sqrt(values.shape[1]))
    return (widened * scale).astype(jnp.bfloat16)


def unit_rows(source, target):
    rows = source.shape[0]
    for start in range(0, rows, STEP):
        part = pl.ds(start, min(STEP, rows - start))
        target[part, :] = unit(source[part, :])


def put(target, start, vector, add):
    for k in range(vector.shape[1] // LANES):
        at = pl.ds(start // LANES + k, 1)
        part = vector[:, k * LANES : (k + 1) * LANES]
        target[at, :] = target[at, :] + part if add else part


def tile_sums(left, right, row_out, row_start, row_add, col_out, col_start, col_add):
    rows, cols = left.shape[0], right.shape[0]
    total = None
    for start in range(0, rows, STEP):
        similarity = lax.dot_general(
            left[pl.ds(start, STEP), :],
            right[...],
            (((1,), (1,)), ((), ())),
            preferred_element_type=jnp.float32,
        )
        value = jnp.exp2(similarity * RATE - RATE)
        folded = value[:, :LANES]
        for k in range(1, cols // LANES):
            folded = folded + value[:, k * LANES : (k + 1) * LANES]
        sums = jnp.sum(folded.T, axis=0, keepdims=True)
        put(row_out, row_start + start, sums, row_add)
        if col_out is not None:
            part = jnp.sum(value.reshape(STEP // 8, 8, cols), axis=0)
            total = part if total is None else total + part
    if col_out is not None:
        put(col_out, col_start, jnp.sum(total, axis=0, keepdims=True), col_add)


def own_kernel(raw, normed, density):
    unit_rows(raw, normed)
    tile_sums(normed, normed, density, 0, False, None, 0, False)


def unit_kernel(raw, normed):
    unit_rows(raw, normed)


def pair_kernel(raw, far, near, to_near, to_far):
    unit_rows(raw, near)
    tile_sums(near, far, to_near, 0, False, to_far, 0, False)


def near_kernel(normed, near, density, to_near, density_out, near_out):
    density_out[...] = density[...]
    near_out[...] = to_near[...]
    tile_sums(normed, near, density_out, 0, True, near_out, 0, True)


def weight_kernel(density, from_near, from_far, weights, total):
    value = 1.0 / (density[...] + from_near[...] + from_far[...])
    weights[...] = value
    total[...] = jnp.full(total.shape, jnp.sum(value))


def scale_kernel(weights, totals, keep, *, rows):
    total = jnp.sum(totals[...], axis=0, keepdims=True)
    keep[...] = weights[...] * rows / total


def call(kernel, operands, outs, scratch=(), flops=0):
    space = pl.BlockSpec(memory_space=pltpu.VMEM)
    shapes = [jax.ShapeDtypeStruct(*out) for out in outs]
    moved = sum(math.prod(s.shape) * s.dtype.itemsize for s in [*operands, *shapes])
    return pl.pallas_call(
        kernel,
        out_shape=shapes,
        in_specs=[space] * len(operands),
        out_specs=[space] * len(shapes),
        scratch_shapes=[pltpu.VMEM(*s) for s in scratch],
        cost_estimate=pl.CostEstimate(
            flops=flops, bytes_accessed=moved, transcendentals=0
        ),
        compiler_params=pltpu.CompilerParams(vmem_limit_bytes=32 * 2**20),
    )(*operands)


def shards(embeddings):
    players = lax.axis_size("dev")
    rows, width = embeddings.shape
    bf16, f32 = jnp.bfloat16, jnp.float32
    block, sums = ((rows, width), bf16), ((rows // LANES, LANES), f32)
    tile = 2 * rows * rows * width
    near_pairs, far_pairs = plan(players)

    near = lax.ppermute(embeddings, "dev", near_pairs)
    far = lax.ppermute(embeddings, "dev", far_pairs)
    normed, density = call(own_kernel, [embeddings], [block, sums], flops=tile)
    (far,) = call(unit_kernel, [far], [block])
    near, to_near, to_far = call(pair_kernel, [near, far], [block, sums, sums], flops=tile)
    from_far = lax.ppermute(to_far, "dev", inverse(far_pairs))
    density, to_near = call(
        near_kernel, [normed, near, density, to_near], [sums, sums], flops=tile
    )
    from_near = lax.ppermute(to_near, "dev", inverse(near_pairs))
    weights, total = call(
        weight_kernel, [density, from_near, from_far], [sums, ((players, LANES), f32)]
    )
    totals = lax.all_to_all(total, "dev", 0, 0, tiled=True)
    (keep,) = call(
        functools.partial(scale_kernel, rows=float(players * rows)), [weights, totals], [sums]
    )
    return keep.reshape(rows)


def solution(mesh):
    return jax.shard_map(
        shards,
        mesh=mesh,
        in_specs=(P("dev", None),),
        out_specs=P("dev"),
        check_vma=False,
    )
```

```python
import functools
import math

import jax
import jax.numpy as jnp
from jax import lax
from jax.experimental import pallas as pl
from jax.experimental.pallas import tpu as pltpu
from jax.sharding import PartitionSpec as P

ROUNDS = 4
LANES = 128
STEP = 256

sharpness = 10.0
RATE = sharpness * math.log2(math.e)


def parity(value):
    return bin(value).count("1") & 1


def plan(players):
    low = players.bit_length() - 1 - ROUNDS
    z_near, z_swap = 1 << low, 3 << low
    x_near, x_swap = 4 << low, 12 << low
    near, far = [], []
    for player in range(players):
        if parity(player >> low) ^ (player & 1):
            near.append((player, player ^ x_near))
            far.append((player, player ^ z_swap))
        else:
            near.append((player, player ^ z_near))
            far.append((player, player ^ x_swap))
    return near, far


def inverse(pairs):
    return [(target, source) for source, target in pairs]


def unit(values):
    widened = values.astype(jnp.float32)
    mean = jnp.mean(widened * widened, axis=1, keepdims=True)
    scale = lax.rsqrt(mean + 1e-06) * (1.0 / math.sqrt(values.shape[1]))
    return (widened * scale).astype(jnp.bfloat16)


def unit_rows(source, target):
    rows = source.shape[0]
    for start in range(0, rows, STEP):
        part = pl.ds(start, min(STEP, rows - start))
        target[part, :] = unit(source[part, :])


def put(target, start, vector, add):
    for k in range(vector.shape[1] // LANES):
        at = pl.ds(start // LANES + k, 1)
        part = vector[:, k * LANES : (k + 1) * LANES]
        target[at, :] = target[at, :] + part if add else part


def tile_sums(left, right, row_out, row_start, row_add, col_out, col_start, col_add):
    rows, cols = left.shape[0], right.shape[0]
    total = None
    for start in range(0, rows, STEP):
        similarity = lax.dot_general(
            left[pl.ds(start, STEP), :],
            right[...],
            (((1,), (1,)), ((), ())),
            preferred_element_type=jnp.float32,
        )
        value = jnp.exp2(similarity * RATE - RATE)
        folded = value[:, :LANES]
        for k in range(1, cols // LANES):
            folded = folded + value[:, k * LANES : (k + 1) * LANES]
        sums = jnp.sum(folded.T, axis=0, keepdims=True)
        put(row_out, row_start + start, sums, row_add)
        if col_out is not None:
            part = jnp.sum(value.reshape(STEP // 8, 8, cols), axis=0)
            total = part if total is None else total + part
    if col_out is not None:
        put(col_out, col_start, jnp.sum(total, axis=0, keepdims=True), col_add)


def own_kernel(raw, normed, density):
    unit_rows(raw, normed)
    tile_sums(normed, normed, density, 0, False, None, 0, False)


def unit_kernel(raw, normed):
    unit_rows(raw, normed)


def pair_kernel(raw, far, near, to_near, to_far):
    unit_rows(raw, near)
    tile_sums(near, far, to_near, 0, False, to_far, 0, False)


def near_kernel(normed, near, density, to_near, density_out, near_out):
    density_out[...] = density[...]
    near_out[...] = to_near[...]
    tile_sums(normed, near, density_out, 0, True, near_out, 0, True)


def add_kernel(density, from_far, out):
    out[...] = density[...] + from_far[...]


def weight_kernel(density, from_near, weights, total):
    value = 1.0 / (density[...] + from_near[...])
    weights[...] = value
    total[...] = jnp.full(total.shape, jnp.sum(value))


def scale_kernel(weights, totals, keep, *, rows):
    total = jnp.sum(totals[...], axis=0, keepdims=True)
    keep[...] = weights[...] * rows / total


def call(kernel, operands, outs, scratch=(), flops=0):
    space = pl.BlockSpec(memory_space=pltpu.VMEM)
    shapes = [jax.ShapeDtypeStruct(*out) for out in outs]
    moved = sum(math.prod(s.shape) * s.dtype.itemsize for s in [*operands, *shapes])
    return pl.pallas_call(
        kernel,
        out_shape=shapes,
        in_specs=[space] * len(operands),
        out_specs=[space] * len(shapes),
        scratch_shapes=[pltpu.VMEM(*s) for s in scratch],
        cost_estimate=pl.CostEstimate(
            flops=flops, bytes_accessed=moved, transcendentals=0
        ),
        compiler_params=pltpu.CompilerParams(vmem_limit_bytes=32 * 2**20),
    )(*operands)


def shards(embeddings):
    players = lax.axis_size("dev")
    rows, width = embeddings.shape
    bf16, f32 = jnp.bfloat16, jnp.float32
    block, sums = ((rows, width), bf16), ((rows // LANES, LANES), f32)
    tile = 2 * rows * rows * width
    near_pairs, far_pairs = plan(players)

    near = lax.ppermute(embeddings, "dev", near_pairs)
    far = lax.ppermute(embeddings, "dev", far_pairs)
    normed, density = call(own_kernel, [embeddings], [block, sums], flops=tile)
    (far,) = call(unit_kernel, [far], [block])
    near, to_near, to_far = call(pair_kernel, [near, far], [block, sums, sums], flops=tile)
    from_far = lax.ppermute(to_far, "dev", inverse(far_pairs))
    density, to_near = call(
        near_kernel, [normed, near, density, to_near], [sums, sums], flops=tile
    )
    from_near = lax.ppermute(to_near, "dev", inverse(near_pairs))
    (density,) = call(add_kernel, [density, from_far], [sums])
    weights, total = call(
        weight_kernel, [density, from_near], [sums, ((players, LANES), f32)]
    )
    totals = lax.all_to_all(total, "dev", 0, 0, tiled=True)
    (keep,) = call(
        functools.partial(scale_kernel, rows=float(players * rows)), [weights, totals], [sums]
    )
    return keep.reshape(rows)


def solution(mesh):
    return jax.shard_map(
        shards,
        mesh=mesh,
        in_specs=(P("dev", None),),
        out_specs=P("dev"),
        check_vma=False,
    )
```

```python
import functools
import math

import jax
import jax.numpy as jnp
from jax import lax
from jax.experimental import pallas as pl
from jax.experimental.pallas import tpu as pltpu
from jax.sharding import PartitionSpec as P

ROUNDS = 4
LANES = 128
STEP = 256
FIRST = 768
COPIES = 4

sharpness = 10.0
RATE = sharpness * math.log2(math.e)


def parity(value):
    return bin(value).count("1") & 1


def plan(players):
    low = players.bit_length() - 1 - ROUNDS
    z_near, z_swap = 1 << low, 3 << low
    x_near, x_swap = 4 << low, 12 << low
    near, far = [], []
    for player in range(players):
        if parity(player >> low) ^ (player & 1):
            near.append((player, player ^ x_near))
            far.append((player, player ^ z_swap))
        else:
            near.append((player, player ^ z_near))
            far.append((player, player ^ x_swap))
    return near, far


def inverse(pairs):
    return [(target, source) for source, target in pairs]


def unit(values):
    widened = values.astype(jnp.float32)
    mean = jnp.mean(widened * widened, axis=1, keepdims=True)
    scale = lax.rsqrt(mean + 1e-06) * (1.0 / math.sqrt(values.shape[1]))
    return (widened * scale).astype(jnp.bfloat16)


def unit_rows(source, target):
    rows = source.shape[0]
    for start in range(0, rows, STEP):
        part = pl.ds(start, min(STEP, rows - start))
        target[part, :] = unit(source[part, :])


def put(target, start, vector, add):
    for k in range(vector.shape[1] // LANES):
        at = pl.ds(start // LANES + k, 1)
        part = vector[:, k * LANES : (k + 1) * LANES]
        target[at, :] = target[at, :] + part if add else part


def tile_sums(left, right, row_out, row_start, row_add, col_out, col_start, col_add):
    rows, cols = left.shape[0], right.shape[0]
    total = None
    for start in range(0, rows, STEP):
        similarity = lax.dot_general(
            left[pl.ds(start, STEP), :],
            right[...],
            (((1,), (1,)), ((), ())),
            preferred_element_type=jnp.float32,
        )
        value = jnp.exp2(similarity * RATE - RATE)
        folded = value[:, :LANES]
        for k in range(1, cols // LANES):
            folded = folded + value[:, k * LANES : (k + 1) * LANES]
        sums = jnp.sum(folded.T, axis=0, keepdims=True)
        put(row_out, row_start + start, sums, row_add)
        if col_out is not None:
            part = jnp.sum(value.reshape(STEP // 8, 8, cols), axis=0)
            total = part if total is None else total + part
    if col_out is not None:
        put(col_out, col_start, jnp.sum(total, axis=0, keepdims=True), col_add)


def take_kernel(raw, taken, sems, *, start):
    rows = taken.shape[0] // COPIES
    copies = [
        pltpu.make_async_copy(
            raw.at[pl.ds(start + k * rows, rows), :],
            taken.at[pl.ds(k * rows, rows), :],
            sems.at[k],
        )
        for k in range(COPIES)
    ]
    for copy in copies:
        copy.start()
    for copy in copies:
        copy.wait()


def own_kernel(first, second, normed, density):
    unit_rows(first, normed.at[pl.ds(0, FIRST), :])
    unit_rows(second, normed.at[pl.ds(FIRST, second.shape[0]), :])
    tile_sums(normed, normed, density, 0, False, None, 0, False)


def unit_kernel(raw, normed):
    unit_rows(raw, normed)


def first_pair_kernel(normed, near_raw, far, density, density_out, near, to_near, to_far):
    unit_rows(near_raw, near)
    density_out[...] = density[...]
    tile_sums(near, far, to_near, 0, False, to_far, 0, False)
    tile_sums(normed, near, density_out, 0, True, to_near, 0, True)


def second_pair_kernel(
    normed, near_first, far_first, near_raw, far_raw, density, to_near, to_far,
    density_out, near_out, far_out, near, far,
):
    unit_rows(near_raw, near)
    unit_rows(far_raw, far)
    density_out[...] = density[...]
    count = FIRST // LANES
    near_out[pl.ds(0, count), :] = to_near[...]
    far_out[pl.ds(0, count), :] = to_far[...]
    tile_sums(normed, near, density_out, 0, True, near_out, FIRST, False)
    tile_sums(near_first, far, near_out, 0, True, far_out, FIRST, False)
    tile_sums(near, far_first, near_out, FIRST, True, far_out, 0, True)
    tile_sums(near, far, near_out, FIRST, True, far_out, FIRST, True)


def weight_kernel(density, from_near, from_far, weights, total):
    value = 1.0 / (density[...] + from_near[...] + from_far[...])
    weights[...] = value
    total[...] = jnp.full(total.shape, jnp.sum(value))


def scale_kernel(weights, totals, keep, *, rows):
    total = jnp.sum(totals[...], axis=0, keepdims=True)
    keep[...] = weights[...] * rows / total


def call(kernel, operands, outs, scratch=(), flops=0, space=pltpu.VMEM, limit=32):
    shapes = [jax.ShapeDtypeStruct(*out) for out in outs]
    moved = sum(math.prod(s.shape) * s.dtype.itemsize for s in [*operands, *shapes])
    return pl.pallas_call(
        kernel,
        out_shape=shapes,
        in_specs=[pl.BlockSpec(memory_space=space)] * len(operands),
        out_specs=[pl.BlockSpec(memory_space=pltpu.VMEM)] * len(shapes),
        scratch_shapes=list(scratch),
        cost_estimate=pl.CostEstimate(
            flops=flops, bytes_accessed=moved, transcendentals=0
        ),
        compiler_params=pltpu.CompilerParams(vmem_limit_bytes=limit * 2**20),
    )(*operands)


def take(rows, start, out):
    (taken,) = call(
        functools.partial(take_kernel, start=start),
        [rows],
        [out],
        [pltpu.SemaphoreType.DMA((COPIES,))],
        space=pltpu.HBM,
        limit=16,
    )
    return taken


def shards(embeddings):
    players = lax.axis_size("dev")
    rows, width = embeddings.shape
    bf16, f32 = jnp.bfloat16, jnp.float32
    block, sums = ((rows, width), bf16), ((rows // LANES, LANES), f32)
    part, rest = ((FIRST, width), bf16), ((rows - FIRST, width), bf16)
    part_sums = ((FIRST // LANES, LANES), f32)
    tile = 2 * rows * rows * width
    near_pairs, far_pairs = plan(players)

    first = take(embeddings, 0, part)
    far_first = lax.ppermute(first, "dev", far_pairs)
    near_first = lax.ppermute(first, "dev", near_pairs)
    second = take(embeddings, FIRST, rest)
    far_second = lax.ppermute(second, "dev", far_pairs)
    near_second = lax.ppermute(second, "dev", near_pairs)
    normed, density = call(own_kernel, [first, second], [block, sums], flops=tile)

    (far_first,) = call(unit_kernel, [far_first], [part])
    density, near_first, to_near, to_far = call(
        first_pair_kernel,
        [normed, near_first, far_first, density],
        [sums, part, part_sums, part_sums],
        flops=tile * 21 // 16,
    )
    density, to_near, to_far = call(
        second_pair_kernel,
        [normed, near_first, far_first, near_second, far_second, density, to_near, to_far],
        [sums, sums, sums],
        [pltpu.VMEM(*rest)] * 2,
        flops=tile * 11 // 16,
    )
    from_near = lax.ppermute(to_near, "dev", inverse(near_pairs))
    from_far = lax.ppermute(to_far, "dev", inverse(far_pairs))
    weights, total = call(
        weight_kernel, [density, from_near, from_far], [sums, ((players, LANES), f32)]
    )
    totals = lax.all_to_all(total, "dev", 0, 0, tiled=True)
    (keep,) = call(
        functools.partial(scale_kernel, rows=float(players * rows)), [weights, totals], [sums]
    )
    return keep.reshape(rows)


def solution(mesh):
    return jax.shard_map(
        shards,
        mesh=mesh,
        in_specs=(P("dev", None),),
        out_specs=P("dev"),
        check_vma=False,
    )
```

```python
import functools
import math

import jax
import jax.numpy as jnp
from jax import lax
from jax.experimental import pallas as pl
from jax.experimental.pallas import tpu as pltpu
from jax.sharding import PartitionSpec as P

ROUNDS = 4
LANES = 128
STEP = 256
FIRST = 768

sharpness = 10.0
RATE = sharpness * math.log2(math.e)


def parity(value):
    return bin(value).count("1") & 1


def plan(players):
    low = players.bit_length() - 1 - ROUNDS
    z_near, z_swap = 1 << low, 3 << low
    x_near, x_swap = 4 << low, 12 << low
    near, far = [], []
    for player in range(players):
        if parity(player >> low) ^ (player & 1):
            near.append((player, player ^ x_near))
            far.append((player, player ^ z_swap))
        else:
            near.append((player, player ^ z_near))
            far.append((player, player ^ x_swap))
    return near, far


def inverse(pairs):
    return [(target, source) for source, target in pairs]


def unit(values):
    widened = values.astype(jnp.float32)
    mean = jnp.mean(widened * widened, axis=1, keepdims=True)
    scale = lax.rsqrt(mean + 1e-06) * (1.0 / math.sqrt(values.shape[1]))
    return (widened * scale).astype(jnp.bfloat16)


def unit_rows(source, target):
    rows = source.shape[0]
    for start in range(0, rows, STEP):
        part = pl.ds(start, min(STEP, rows - start))
        target[part, :] = unit(source[part, :])


def put(target, start, vector, add):
    for k in range(vector.shape[1] // LANES):
        at = pl.ds(start // LANES + k, 1)
        part = vector[:, k * LANES : (k + 1) * LANES]
        target[at, :] = target[at, :] + part if add else part


def tile_sums(left, right, row_out, row_start, row_add, col_out, col_start, col_add):
    rows, cols = left.shape[0], right.shape[0]
    total = None
    for start in range(0, rows, STEP):
        similarity = lax.dot_general(
            left[pl.ds(start, STEP), :],
            right[...],
            (((1,), (1,)), ((), ())),
            preferred_element_type=jnp.float32,
        )
        value = jnp.exp2(similarity * RATE - RATE)
        folded = value[:, :LANES]
        for k in range(1, cols // LANES):
            folded = folded + value[:, k * LANES : (k + 1) * LANES]
        sums = jnp.sum(folded.T, axis=0, keepdims=True)
        put(row_out, row_start + start, sums, row_add)
        if col_out is not None:
            part = jnp.sum(value.reshape(STEP // 8, 8, cols), axis=0)
            total = part if total is None else total + part
    if col_out is not None:
        put(col_out, col_start, jnp.sum(total, axis=0, keepdims=True), col_add)


def own_kernel(first, second, normed, density):
    unit_rows(first, normed.at[pl.ds(0, FIRST), :])
    unit_rows(second, normed.at[pl.ds(FIRST, second.shape[0]), :])
    tile_sums(normed, normed, density, 0, False, None, 0, False)


def unit_kernel(raw, normed):
    unit_rows(raw, normed)


def first_pair_kernel(normed, near_raw, far, density, density_out, near, to_near, to_far):
    unit_rows(near_raw, near)
    density_out[...] = density[...]
    tile_sums(near, far, to_near, 0, False, to_far, 0, False)
    tile_sums(normed, near, density_out, 0, True, to_near, 0, True)


def second_pair_kernel(
    normed, near_first, far_first, near_raw, far_raw, density, to_near, to_far,
    density_out, near_out, far_out, near, far,
):
    unit_rows(near_raw, near)
    unit_rows(far_raw, far)
    density_out[...] = density[...]
    count = FIRST // LANES
    near_out[pl.ds(0, count), :] = to_near[...]
    far_out[pl.ds(0, count), :] = to_far[...]
    tile_sums(normed, near, density_out, 0, True, near_out, FIRST, False)
    tile_sums(near_first, far, near_out, 0, True, far_out, FIRST, False)
    tile_sums(near, far_first, near_out, FIRST, True, far_out, 0, True)
    tile_sums(near, far, near_out, FIRST, True, far_out, FIRST, True)


def weight_kernel(density, from_near, from_far, weights, total):
    value = 1.0 / (density[...] + from_near[...] + from_far[...])
    weights[...] = value
    total[...] = jnp.full(total.shape, jnp.sum(value))


def scale_kernel(weights, totals, keep, *, rows):
    total = jnp.sum(totals[...], axis=0, keepdims=True)
    keep[...] = weights[...] * rows / total


def call(kernel, operands, outs, scratch=(), flops=0):
    shapes = [jax.ShapeDtypeStruct(*out) for out in outs]
    moved = sum(math.prod(s.shape) * s.dtype.itemsize for s in [*operands, *shapes])
    return pl.pallas_call(
        kernel,
        out_shape=shapes,
        in_specs=[pl.BlockSpec(memory_space=pltpu.VMEM)] * len(operands),
        out_specs=[pl.BlockSpec(memory_space=pltpu.VMEM)] * len(shapes),
        scratch_shapes=list(scratch),
        cost_estimate=pl.CostEstimate(
            flops=flops, bytes_accessed=moved, transcendentals=0
        ),
        compiler_params=pltpu.CompilerParams(vmem_limit_bytes=32 * 2**20),
    )(*operands)


def shards(embeddings):
    players = lax.axis_size("dev")
    rows, width = embeddings.shape
    bf16, f32 = jnp.bfloat16, jnp.float32
    block, sums = ((rows, width), bf16), ((rows // LANES, LANES), f32)
    part, rest = ((FIRST, width), bf16), ((rows - FIRST, width), bf16)
    part_sums = ((FIRST // LANES, LANES), f32)
    tile = 2 * rows * rows * width
    near_pairs, far_pairs = plan(players)

    first = embeddings[:FIRST]
    far_first = lax.ppermute(first, "dev", far_pairs)
    near_first = lax.ppermute(first, "dev", near_pairs)
    second = embeddings[FIRST:]
    far_second = lax.ppermute(second, "dev", far_pairs)
    near_second = lax.ppermute(second, "dev", near_pairs)
    normed, density = call(own_kernel, [first, second], [block, sums], flops=tile)

    (far_first,) = call(unit_kernel, [far_first], [part])
    density, near_first, to_near, to_far = call(
        first_pair_kernel,
        [normed, near_first, far_first, density],
        [sums, part, part_sums, part_sums],
        flops=tile * 21 // 16,
    )
    density, to_near, to_far = call(
        second_pair_kernel,
        [normed, near_first, far_first, near_second, far_second, density, to_near, to_far],
        [sums, sums, sums],
        [pltpu.VMEM(*rest)] * 2,
        flops=tile * 11 // 16,
    )
    from_near = lax.ppermute(to_near, "dev", inverse(near_pairs))
    from_far = lax.ppermute(to_far, "dev", inverse(far_pairs))
    weights, total = call(
        weight_kernel, [density, from_near, from_far], [sums, ((players, LANES), f32)]
    )
    totals = lax.all_to_all(total, "dev", 0, 0, tiled=True)
    (keep,) = call(
        functools.partial(scale_kernel, rows=float(players * rows)), [weights, totals], [sums]
    )
    return keep.reshape(rows)


def solution(mesh):
    return jax.shard_map(
        shards,
        mesh=mesh,
        in_specs=(P("dev", None),),
        out_specs=P("dev"),
        check_vma=False,
    )
```

```python
import functools
import math

import jax
import jax.numpy as jnp
import numpy as np
from jax import lax
from jax.experimental import pallas as pl
from jax.experimental.pallas import tpu as pltpu
from jax.sharding import PartitionSpec as P

ROUNDS = 4
LANES = 128
STEP = 256
FIRST = 768

sharpness = 10.0
RATE = sharpness * math.log2(math.e)


def parity(value):
    return bin(value).count("1") & 1


def plan(players):
    low = players.bit_length() - 1 - ROUNDS
    z_near, z_swap = 1 << low, 3 << low
    x_near, x_swap = 4 << low, 12 << low
    near, far = [], []
    for player in range(players):
        if parity(player >> low) ^ (player & 1):
            near.append((player, player ^ x_near))
            far.append((player, player ^ z_swap))
        else:
            near.append((player, player ^ z_near))
            far.append((player, player ^ x_swap))
    return near, far


def inverse(pairs):
    return [(target, source) for source, target in pairs]


def unit(values):
    widened = values.astype(jnp.float32)
    mean = jnp.mean(widened * widened, axis=1, keepdims=True)
    scale = lax.rsqrt(mean + 1e-06) * (1.0 / math.sqrt(values.shape[1]))
    return (widened * scale).astype(jnp.bfloat16)


def unit_rows(source, target):
    rows = source.shape[0]
    for start in range(0, rows, STEP):
        part = pl.ds(start, min(STEP, rows - start))
        target[part, :] = unit(source[part, :])


def put(target, start, vector, add):
    for k in range(vector.shape[1] // LANES):
        at = pl.ds(start // LANES + k, 1)
        part = vector[:, k * LANES : (k + 1) * LANES]
        target[at, :] = target[at, :] + part if add else part


def tile_sums(left, right, row_out, row_start, row_add, col_out, col_start, col_add):
    rows, cols = left.shape[0], right.shape[0]
    total = None
    for start in range(0, rows, STEP):
        similarity = lax.dot_general(
            left[pl.ds(start, STEP), :],
            right[...],
            (((1,), (1,)), ((), ())),
            preferred_element_type=jnp.float32,
        )
        value = jnp.exp2(similarity * RATE - RATE)
        folded = value[:, :LANES]
        for k in range(1, cols // LANES):
            folded = folded + value[:, k * LANES : (k + 1) * LANES]
        sums = jnp.sum(folded.T, axis=0, keepdims=True)
        put(row_out, row_start + start, sums, row_add)
        if col_out is not None:
            part = jnp.sum(value.reshape(STEP // 8, 8, cols), axis=0)
            total = part if total is None else total + part
    if col_out is not None:
        put(col_out, col_start, jnp.sum(total, axis=0, keepdims=True), col_add)


def own_kernel(first, second, normed, density):
    unit_rows(first, normed.at[pl.ds(0, FIRST), :])
    unit_rows(second, normed.at[pl.ds(FIRST, second.shape[0]), :])
    tile_sums(normed, normed, density, 0, False, None, 0, False)


def unit_kernel(raw, normed):
    unit_rows(raw, normed)


def first_pair_kernel(normed, near_raw, far, density, density_out, near, to_near, to_far):
    unit_rows(near_raw, near)
    density_out[...] = density[...]
    tile_sums(near, far, to_near, 0, False, to_far, 0, False)
    tile_sums(normed, near, density_out, 0, True, to_near, 0, True)


def second_pair_kernel(
    normed, near_first, far_first, near_raw, far_raw, density, to_near, to_far,
    density_out, near_out, far_out, near, far,
):
    unit_rows(near_raw, near)
    unit_rows(far_raw, far)
    density_out[...] = density[...]
    count = FIRST // LANES
    near_out[pl.ds(0, count), :] = to_near[...]
    far_out[pl.ds(0, count), :] = to_far[...]
    tile_sums(normed, near, density_out, 0, True, near_out, FIRST, False)
    tile_sums(near_first, far, near_out, 0, True, far_out, FIRST, False)
    tile_sums(near, far_first, near_out, FIRST, True, far_out, 0, True)
    tile_sums(near, far, near_out, FIRST, True, far_out, FIRST, True)


def weight_kernel(density, from_near, from_far, weights, total):
    value = 1.0 / (density[...] + from_near[...] + from_far[...])
    weights[...] = value
    total[...] = jnp.full(total.shape, jnp.sum(value))


def scale_kernel(weights, totals, keep, *, rows):
    total = jnp.sum(totals[...], axis=0, keepdims=True)
    keep[...] = weights[...] * rows / total


def call(kernel, operands, outs, scratch=(), flops=0):
    shapes = [jax.ShapeDtypeStruct(*out) for out in outs]
    moved = sum(math.prod(s.shape) * s.dtype.itemsize for s in [*operands, *shapes])
    return pl.pallas_call(
        kernel,
        out_shape=shapes,
        in_specs=[pl.BlockSpec(memory_space=pltpu.VMEM)] * len(operands),
        out_specs=[pl.BlockSpec(memory_space=pltpu.VMEM)] * len(shapes),
        scratch_shapes=list(scratch),
        cost_estimate=pl.CostEstimate(
            flops=flops, bytes_accessed=moved, transcendentals=0
        ),
        compiler_params=pltpu.CompilerParams(vmem_limit_bytes=32 * 2**20),
    )(*operands)


def shards(embeddings):
    players = lax.axis_size("dev")
    rows, width = embeddings.shape
    bf16, f32 = jnp.bfloat16, jnp.float32
    block, sums = ((rows, width), bf16), ((rows // LANES, LANES), f32)
    part, rest = ((FIRST, width), bf16), ((rows - FIRST, width), bf16)
    part_sums = ((FIRST // LANES, LANES), f32)
    tile = 2 * rows * rows * width
    near_pairs, far_pairs = plan(players)

    first = embeddings[:FIRST]
    far_first = lax.ppermute(first, "dev", far_pairs)
    near_first = lax.ppermute(first, "dev", near_pairs)
    second = embeddings[FIRST:]
    far_second = lax.ppermute(second, "dev", far_pairs)
    near_second = lax.ppermute(second, "dev", near_pairs)
    normed, density = call(own_kernel, [first, second], [block, sums], flops=tile)

    (far_first,) = call(unit_kernel, [far_first], [part])
    density, near_first, to_near, to_far = call(
        first_pair_kernel,
        [normed, near_first, far_first, density],
        [sums, part, part_sums, part_sums],
        flops=tile * 21 // 16,
    )
    density, to_near, to_far = call(
        second_pair_kernel,
        [normed, near_first, far_first, near_second, far_second, density, to_near, to_far],
        [sums, sums, sums],
        [pltpu.VMEM(*rest)] * 2,
        flops=tile * 11 // 16,
    )
    from_near = lax.ppermute(to_near, "dev", inverse(near_pairs))
    from_far = lax.ppermute(to_far, "dev", inverse(far_pairs))
    weights, total = call(
        weight_kernel, [density, from_near, from_far], [sums, ((players, LANES), f32)]
    )
    order = [int(peer) for peer in np.random.default_rng(1).permutation(players)]
    totals = lax.all_to_all(
        total, "dev", 0, 0, axis_index_groups=[order], tiled=True
    )
    (keep,) = call(
        functools.partial(scale_kernel, rows=float(players * rows)), [weights, totals], [sums]
    )
    return keep.reshape(rows)


def solution(mesh):
    return jax.shard_map(
        shards,
        mesh=mesh,
        in_specs=(P("dev", None),),
        out_specs=P("dev"),
        check_vma=False,
    )
```

```python
import functools
import math

import jax
import jax.numpy as jnp
import numpy as np
from jax import lax
from jax.experimental import pallas as pl
from jax.experimental.pallas import tpu as pltpu
from jax.sharding import PartitionSpec as P

ROUNDS = 4
LANES = 128
STEP = 256
FIRST = 768

sharpness = 10.0
RATE = sharpness * math.log2(math.e)


def parity(value):
    return bin(value).count("1") & 1


def plan(players):
    low = players.bit_length() - 1 - ROUNDS
    z_near, z_swap = 1 << low, 3 << low
    x_near, x_swap = 4 << low, 12 << low
    near, far = [], []
    for player in range(players):
        if parity(player >> low) ^ (player & 1):
            near.append((player, player ^ x_near))
            far.append((player, player ^ z_swap))
        else:
            near.append((player, player ^ z_near))
            far.append((player, player ^ x_swap))
    return near, far


def inverse(pairs):
    return [(target, source) for source, target in pairs]


def unit(values):
    widened = values.astype(jnp.float32)
    mean = jnp.mean(widened * widened, axis=1, keepdims=True)
    scale = lax.rsqrt(mean + 1e-06) * (1.0 / math.sqrt(values.shape[1]))
    return (widened * scale).astype(jnp.bfloat16)


def unit_rows(source, target):
    rows = source.shape[0]
    for start in range(0, rows, STEP):
        part = pl.ds(start, min(STEP, rows - start))
        target[part, :] = unit(source[part, :])


def put(target, start, vector, add):
    for k in range(vector.shape[1] // LANES):
        at = pl.ds(start // LANES + k, 1)
        part = vector[:, k * LANES : (k + 1) * LANES]
        target[at, :] = target[at, :] + part if add else part


def tile_sums(left, right, row_out, row_start, row_add, col_out, col_start, col_add):
    rows, cols = left.shape[0], right.shape[0]
    total = None
    for start in range(0, rows, STEP):
        similarity = lax.dot_general(
            left[pl.ds(start, STEP), :],
            right[...],
            (((1,), (1,)), ((), ())),
            preferred_element_type=jnp.float32,
        )
        value = jnp.exp2(similarity * RATE - RATE)
        folded = value[:, :LANES]
        for k in range(1, cols // LANES):
            folded = folded + value[:, k * LANES : (k + 1) * LANES]
        sums = jnp.sum(folded.T, axis=0, keepdims=True)
        put(row_out, row_start + start, sums, row_add)
        if col_out is not None:
            part = jnp.sum(value.reshape(STEP // 8, 8, cols), axis=0)
            total = part if total is None else total + part
    if col_out is not None:
        put(col_out, col_start, jnp.sum(total, axis=0, keepdims=True), col_add)


def own_kernel(first, second, normed, density):
    unit_rows(first, normed.at[pl.ds(0, FIRST), :])
    unit_rows(second, normed.at[pl.ds(FIRST, second.shape[0]), :])
    tile_sums(normed, normed, density, 0, False, None, 0, False)


def unit_kernel(raw, normed):
    unit_rows(raw, normed)


def first_pair_kernel(normed, near_raw, far, density, density_out, near, to_near, to_far):
    unit_rows(near_raw, near)
    density_out[...] = density[...]
    tile_sums(near, far, to_near, 0, False, to_far, 0, False)
    tile_sums(normed, near, density_out, 0, True, to_near, 0, True)


def second_pair_kernel(
    normed, near_first, far_first, near_raw, far_raw, density, to_near, to_far,
    density_out, near_out, far_out, near, far,
):
    unit_rows(near_raw, near)
    unit_rows(far_raw, far)
    density_out[...] = density[...]
    count = FIRST // LANES
    near_out[pl.ds(0, count), :] = to_near[...]
    far_out[pl.ds(0, count), :] = to_far[...]
    tile_sums(normed, near, density_out, 0, True, near_out, FIRST, False)
    tile_sums(near_first, far, near_out, 0, True, far_out, FIRST, False)
    tile_sums(near, far_first, near_out, FIRST, True, far_out, 0, True)
    tile_sums(near, far, near_out, FIRST, True, far_out, FIRST, True)


def weight_kernel(density, from_near, from_far, weights, total):
    value = 1.0 / (density[...] + from_near[...] + from_far[...])
    weights[...] = value
    total[...] = jnp.full(total.shape, jnp.sum(value))


def scale_kernel(weights, totals, keep, *, rows):
    total = jnp.sum(totals[...], axis=0, keepdims=True)[:, :1]
    keep[...] = weights[...] * rows / total


def call(kernel, operands, outs, scratch=(), flops=0):
    shapes = [jax.ShapeDtypeStruct(*out) for out in outs]
    moved = sum(math.prod(s.shape) * s.dtype.itemsize for s in [*operands, *shapes])
    return pl.pallas_call(
        kernel,
        out_shape=shapes,
        in_specs=[pl.BlockSpec(memory_space=pltpu.VMEM)] * len(operands),
        out_specs=[pl.BlockSpec(memory_space=pltpu.VMEM)] * len(shapes),
        scratch_shapes=list(scratch),
        cost_estimate=pl.CostEstimate(
            flops=flops, bytes_accessed=moved, transcendentals=0
        ),
        compiler_params=pltpu.CompilerParams(vmem_limit_bytes=32 * 2**20),
    )(*operands)


def shards(embeddings):
    players = lax.axis_size("dev")
    rows, width = embeddings.shape
    bf16, f32 = jnp.bfloat16, jnp.float32
    block, sums = ((rows, width), bf16), ((rows // LANES, LANES), f32)
    part, rest = ((FIRST, width), bf16), ((rows - FIRST, width), bf16)
    part_sums = ((FIRST // LANES, LANES), f32)
    tile = 2 * rows * rows * width
    near_pairs, far_pairs = plan(players)

    first = embeddings[:FIRST]
    far_first = lax.ppermute(first, "dev", far_pairs)
    near_first = lax.ppermute(first, "dev", near_pairs)
    second = embeddings[FIRST:]
    far_second = lax.ppermute(second, "dev", far_pairs)
    near_second = lax.ppermute(second, "dev", near_pairs)
    normed, density = call(own_kernel, [first, second], [block, sums], flops=tile)

    (far_first,) = call(unit_kernel, [far_first], [part])
    density, near_first, to_near, to_far = call(
        first_pair_kernel,
        [normed, near_first, far_first, density],
        [sums, part, part_sums, part_sums],
        flops=tile * 21 // 16,
    )
    density, to_near, to_far = call(
        second_pair_kernel,
        [normed, near_first, far_first, near_second, far_second, density, to_near, to_far],
        [sums, sums, sums],
        [pltpu.VMEM(*rest)] * 2,
        flops=tile * 11 // 16,
    )
    from_near = lax.ppermute(to_near, "dev", inverse(near_pairs))
    from_far = lax.ppermute(to_far, "dev", inverse(far_pairs))
    weights, total = call(
        weight_kernel, [density, from_near, from_far], [sums, ((players, 8), f32)]
    )
    order = [int(peer) for peer in np.random.default_rng(1).permutation(players)]
    totals = lax.all_to_all(
        total, "dev", 0, 0, axis_index_groups=[order], tiled=True
    )
    (keep,) = call(
        functools.partial(scale_kernel, rows=float(players * rows)), [weights, totals], [sums]
    )
    return keep.reshape(rows)


def solution(mesh):
    return jax.shard_map(
        shards,
        mesh=mesh,
        in_specs=(P("dev", None),),
        out_specs=P("dev"),
        check_vma=False,
    )
```
